32 devices in a mesh: rep: 2 (over x), shard: 16 (over z, y, core).
Axes of the slice: x: 2, y: 2, z: 4, core: 2. Of those that a mesh axis runs over, the one named last changes fastest.
Arguments:
- theta: float32 [12, 1024, 1024], P(None, 'shard')
- inner: bfloat16 [2, 12, 1024, 1024], P('rep', None, 'shard'), may hold values from -6 to 6
- momentum: float32 [32, 1024, 1024], P('shard'), may hold values from -6 to 6
- owner: int32 [12], replicated, may hold values from 0 to 15, as said below
- order: int32 [3, 4], replicated, may hold values from 0 to 3, as said below
Outputs:
- new_theta: float32 [12, 1024, 1024], P(None, 'shard')
- new_momentum: float32 [32, 1024, 1024], P('shard')
The draws below stay inside these ranges and needn't reach their ends.
Inputs may be any that keep to these rules, and one draw needn't show every extreme that they name: No owner is named by more than 2 projections, and some owner is named by exactly 2. `order`: each row is a permutation of 0, 1, 2, 3.
All inputs are finite; a program needn't handle non-finite values.
Results may differ from the reference program's by a relative error of at most 0.0003.
Values sent between devices are 32-bit elements; how exact they have to be, the bound alone decides.
No kernel may reach another device: no remote copies, remote signals or barrier semaphores. Data moves between devices by JAX's collectives and lax.ppermute only.
A program may use at most 128 MiB of HBM per device.

```python
import math
import jax
import jax.numpy as jnp
from jax import lax

D = 1024
CAP = 2
LAYERS = 3
MATS = 12
SLOTS = 32
N_REP = 2


def draw_theta(key, part):
    keys = jax.random.split(key, 3)
    row_scale = jnp.exp(jax.random.uniform(keys[1], (MATS, D, 1), jnp.float32, math.log(0.3), math.log(3.0)))
    col_scale = jnp.exp(jax.random.uniform(keys[2], (MATS, 1, D), jnp.float32, math.log(0.3), math.log(3.0)))
    base = jax.random.normal(keys[0], (MATS, D, D), jnp.float32)
    return (base * row_scale * col_scale).astype(jnp.float32)


def draw_owner(key, part):
    keys = jax.random.split(key, 2)
    seq = jax.random.permutation(keys[0], SLOTS).astype(jnp.int32)
    inverse = jnp.argsort(seq).astype(jnp.int32)
    first = seq[0]
    partner = first - first % CAP + (first % CAP + 1) % CAP
    score = 2 * inverse + 1
    score = jnp.where(jnp.arange(SLOTS, dtype=jnp.int32) == partner, 2, score)
    picked = jnp.argsort(score).astype(jnp.int32)[:MATS] // CAP
    offset = jax.random.randint(keys[1], (), 0, MATS)
    return jnp.roll(picked, offset).astype(jnp.int32)


def draw_order(key, part):
    keys = jax.random.split(key, LAYERS)
    return jax.vmap(lambda k: jax.random.permutation(k, 4))(keys).astype(jnp.int32)


def level_of(own_key, dims, cuts, low, top_value):
    def one(axis_at, blocks):
        heights = jax.random.uniform(jax.random.fold_in(jax.random.fold_in(own_key, 6), axis_at), (blocks,), jnp.float32, low / len(cuts), top_value / len(cuts))
        return jnp.repeat(jnp.exp(heights), dims[axis_at] // blocks).reshape((-1,) + (1,) * (len(dims) - axis_at - 1))

    gain = one(*cuts[0])
    for cut in cuts[1:]:
        gain = gain * one(*cut)
    return gain


def scatter_about(rng, shape, width, limit, cuts=(), kind=jnp.bfloat16):
    entries = width * jax.random.normal(rng, shape, jnp.float32)
    if cuts:
        entries = entries * level_of(rng, shape, cuts, -0.22, 0.18)
    return jnp.clip(entries, -limit, limit).astype(kind)


def setup_inputs(seed: int = 0) -> dict:
    key_list = jax.random.split(jax.random.key(seed), 6)
    return {
        "theta": draw_theta(jax.random.fold_in(key_list[5], 71), 0),
        "inner": scatter_about(key_list[1], (N_REP, MATS, D, D), 1.0, 6.0, ((0, 2), (2, 16))),
        "momentum": scatter_about(key_list[2], (SLOTS, D, D), 1.0, 6.0, ((0, 16),), jnp.float32),
        "owner": draw_owner(jax.random.fold_in(key_list[5], 71), 0),
        "order": draw_order(jax.random.fold_in(key_list[5], 71), 0),
    }


def reference(theta, inner, momentum, owner, order):
    ident = (4 * jnp.arange(LAYERS, dtype=jnp.int32)[:, None] + order).reshape(MATS).astype(jnp.int32)
    mat_ids = jnp.arange(MATS, dtype=jnp.int32)
    same = owner[:, None] == owner[None, :]
    earlier = mat_ids[None, :] < mat_ids[:, None]
    rank = lax.optimization_barrier(jnp.sum((same & earlier).astype(jnp.int32), axis=1))
    slot = (CAP * owner + rank).astype(jnp.int32)
    slot_pos = slot[ident]
    summed = jnp.zeros(theta.shape, jnp.float32)
    for group in range(N_REP):
        summed = summed + (theta - inner[group].astype(jnp.float32))
    outer = summed / N_REP
    fresh = 0.5 * momentum[slot_pos] + outer
    new_momentum = momentum.at[slot_pos].set(fresh)
    shifted = theta - 0.7 * (outer + 0.5 * fresh)
    new_theta = shifted / jnp.sqrt(lax.optimization_barrier(jnp.mean(shifted * shifted, axis=-1, keepdims=True)) + 1e-06)
    return (new_theta, new_momentum)
```

```python
import functools

import jax
import jax.numpy as jnp
from jax import lax
from jax.experimental import pallas as pl
from jax.experimental.pallas import tpu as pltpu
from jax.sharding import PartitionSpec as P

CORES = 2
CHIP = 3
REP = 1


def whole(shape):
    return pl.BlockSpec(shape, lambda *_: (0,) * len(shape))


def params(*arrays):
    size = sum(a.size * 4 for a in arrays)
    return pltpu.CompilerParams(vmem_limit_bytes=min(60 << 20, (8 << 20) + 3 * size))


def pack_momentum(meta, table, momentum6, crossed, chunk, rows, cap):
    ranks, chips, _, _, _, width = momentum6.shape

    def kernel(meta_ref, table_ref, own_ref, crossed_ref, *outs):
        chip, core = meta_ref[0], meta_ref[1]
        for slot in range(cap):
            entry = chip * 4 + slot
            rank = table_ref[1, entry]
            mine = table_ref[2, entry] == core
            for dist in range(chips):
                other = chip ^ dist

                @pl.when(mine)
                def _():
                    outs[dist][slot] = own_ref[rank, other, 0, 0]

                @pl.when(jnp.logical_not(mine))
                def _():
                    outs[dist][slot] = crossed_ref[rank, other]

    out = jax.ShapeDtypeStruct((cap, rows, width), jnp.float32)
    own_block = (ranks, chips, 1, 1, rows, width)
    block_at = lambda i, meta_ref, table_ref: (0, 0, meta_ref[1], meta_ref[2], chunk, 0)
    return pl.pallas_call(
        kernel,
        grid_spec=pltpu.PrefetchScalarGridSpec(
            num_scalar_prefetch=2,
            grid=(1,),
            in_specs=[pl.BlockSpec(own_block, block_at), whole(crossed.shape)],
            out_specs=[whole(out.shape)] * chips,
        ),
        out_shape=[out] * chips,
        compiler_params=params(crossed, crossed, *[out] * chips),
        name="pack_momentum",
    )(meta, table, momentum6, crossed)


def pack_outer(meta, table, mine, theirs, chips, groups, chunk, cap):
    mats, rows, width = mine.shape
    count = rows // chunk

    def kernel(meta_ref, table_ref, mine_ref, theirs_ref, outer_ref, *outs):
        outer_ref[...] = (mine_ref[...] + theirs_ref[...]) / groups
        chip = meta_ref[0]
        for dist in range(chips):
            for slot in range(cap):
                at = table_ref[0, (chip ^ dist) * 4 + slot]
                for i in range(count):
                    outs[i * chips + dist][slot] = outer_ref[at, i * chunk : (i + 1) * chunk]

    out = jax.ShapeDtypeStruct((cap, chunk, width), jnp.float32)
    outer, *sent = pl.pallas_call(
        kernel,
        grid_spec=pltpu.PrefetchScalarGridSpec(
            num_scalar_prefetch=2,
            grid=(1,),
            in_specs=[whole(mine.shape), whole(mine.shape)],
            out_specs=[whole(mine.shape)] + [whole(out.shape)] * (count * chips),
        ),
        out_shape=[jax.ShapeDtypeStruct(mine.shape, jnp.float32)] + [out] * (count * chips),
        compiler_params=params(mine, mine, mine, *[out] * (count * chips)),
        name="pack_outer",
    )(meta, table, mine, theirs)
    return outer, [sent[i * chips : (i + 1) * chips] for i in range(count)]


def join(blocks):
    def kernel(*refs):
        for i in range(len(blocks)):
            refs[-1][i] = refs[i][...]

    block = blocks[0]
    return pl.pallas_call(
        kernel,
        out_shape=jax.ShapeDtypeStruct((len(blocks), *block.shape), jnp.float32),
        in_specs=[pl.BlockSpec(memory_space=pltpu.VMEM)] * len(blocks),
        out_specs=pl.BlockSpec(memory_space=pltpu.VMEM),
        compiler_params=params(*blocks),
        name="join",
    )(*blocks)


def step_theta(meta, table, theta4, outer, blocks, chunk, rows, cap):
    mats, _, _, width = theta4.shape
    chips = len(blocks)

    def kernel(meta_ref, table_ref, theta_ref, outer_ref, *refs):
        out_ref = refs[chips]
        chip = meta_ref[0]
        for dist in range(chips):
            for slot in range(cap):
                entry = (chip ^ dist) * 4 + slot

                @pl.when(table_ref[3, entry] > 0)
                def _():
                    at = table_ref[0, entry]
                    outer_now = outer_ref[at]
                    fresh = 0.5 * refs[dist][slot] + outer_now
                    shifted = theta_ref[at, 0] - 0.7 * (outer_now + 0.5 * fresh)
                    mean = jnp.mean(shifted * shifted, axis=-1, keepdims=True)
                    out_ref[at] = shifted / jnp.sqrt(mean + 1e-06)

    out = jax.ShapeDtypeStruct((mats, rows, width), jnp.float32)
    return pl.pallas_call(
        kernel,
        grid_spec=pltpu.PrefetchScalarGridSpec(
            num_scalar_prefetch=2,
            grid=(1,),
            in_specs=[
                pl.BlockSpec((mats, 1, rows, width), lambda i, meta_ref, table_ref: (0, meta_ref[2], chunk, 0)),
                pl.BlockSpec((mats, rows, width), lambda i, meta_ref, table_ref: (0, chunk, 0)),
            ]
            + [whole((cap, rows, width))] * chips,
            out_specs=whole(out.shape),
        ),
        out_shape=out,
        compiler_params=params(out, out, out, *blocks),
        name="step_theta",
    )(meta, table, theta4, outer, *blocks)


def step_momentum(meta, held, momentum6, near, far, old, chunk, own_half):
    ranks, chips, _, _, _, width = momentum6.shape
    rows = near.shape[2]

    def kernel(meta_ref, held_ref, momentum_ref, near_ref, far_ref, *refs):
        out_ref = refs[-1]
        chip, core = meta_ref[0], meta_ref[1]
        used = held_ref[1, pl.program_id(0)] > 0

        @pl.when(used)
        def _():
            for at in range(chips):
                for place, ref in ((core, near_ref), (1 - core, far_ref)):
                    out_ref[0, at, place, 0] = 0.5 * momentum_ref[0, at, place, 0] + ref[at ^ chip, 0]

        @pl.when(jnp.logical_not(used))
        def _():
            out_ref[...] = momentum_ref[...]

    def big_at(k, meta_ref, held_ref):
        return k, 0, 0, meta_ref[2] if own_half else 1 - meta_ref[2], chunk, 0

    big = pl.BlockSpec((1, chips, CORES, 1, rows, width), big_at)
    small = pl.BlockSpec((chips, 1, rows, width), lambda k, meta_ref, held_ref: (0, held_ref[0, k], 0, 0))
    extra = [] if old is None else [old]
    size = chips * CORES * rows * width * 4
    return pl.pallas_call(
        kernel,
        grid_spec=pltpu.PrefetchScalarGridSpec(
            num_scalar_prefetch=2,
            grid=(ranks,),
            in_specs=[big, small, small] + [pl.BlockSpec(memory_space=pl.ANY)] * len(extra),
            out_specs=big,
        ),
        out_shape=jax.ShapeDtypeStruct(momentum6.shape, jnp.float32),
        input_output_aliases={5: 0} if extra else {},
        compiler_params=pltpu.CompilerParams(vmem_limit_bytes=(8 << 20) + 6 * size),
        name="step_momentum",
    )(meta, held, momentum6, near, far, *extra)


def swap_core(x):
    owners = lax.axis_size("shard")
    with jax.named_scope("swap_core"):
        return lax.ppermute(x, "shard", [(s, s ^ 1) for s in range(owners)])


def cross_momentum(momentum, half, chunk):
    owners = lax.axis_size("shard")
    ranks, _, width = momentum.shape
    chips = owners // CORES
    groups = lax.axis_size("rep")
    momentum6 = momentum.reshape(ranks, chips, CORES, groups, half, width)
    other = 1 - lax.axis_index("shard") % CORES
    out = []
    for first in range(0, half, chunk):
        start = (0, 0, other, lax.axis_index("rep"), first, 0)
        part = lax.dynamic_slice(momentum6, start, (ranks, chips, 1, 1, chunk, width))
        out.append(swap_core(part.reshape(ranks, chips, chunk, width)))
    return out


def after(x, *done):
    return lax.optimization_barrier((x, *done))[0]


class Lane:
    def __init__(self, window, send):
        self.window, self.send, self.arrived = window, send, []

    def __call__(self, x, *args):
        if len(self.arrived) >= self.window:
            x = after(x, self.arrived[-self.window])
        self.arrived.append(self.send(x, *args))
        return self.arrived[-1]


def run(cap, theta, inner, momentum, crossed, meta, table, held):
    groups = lax.axis_size("rep")
    owners = lax.axis_size("shard")
    chips = owners // CORES
    mats, rows, width = theta.shape
    ranks = momentum.shape[0]
    half = rows // groups
    rep = lax.axis_index("rep")

    def swap_rep(x):
        with jax.named_scope("swap_rep"):
            return lax.ppermute(x, "rep", [(g, g ^ 1) for g in range(groups)])

    def swap_chip(x, dist):
        with jax.named_scope(f"swap_chip_{dist}"):
            return lax.ppermute(x, "shard", [(s, s ^ (CORES * dist)) for s in range(owners)])

    lane = Lane(CHIP, swap_chip)
    rep_lane = Lane(REP, swap_rep)
    half_way = chips // 2
    order = [d for pair in zip(range(half_way, chips), range(1, half_way + 1)) for d in pair]
    order.remove(half_way)
    order = [half_way] + [d for d in order if d != half_way]

    theta4 = theta.reshape(mats, groups, half, width)
    inner4 = inner.reshape(mats, groups, half, width)
    momentum6 = momentum.reshape(ranks, chips, CORES, groups, half, width)
    count = len(crossed)
    chunk = half // count

    def diff(at):
        pick = lambda a: lax.dynamic_index_in_dim(a, at, 1, keepdims=False)
        return pick(theta4) - pick(inner4).astype(jnp.float32)

    theirs = rep_lane(diff(1 - rep))
    mine = diff(rep)

    def spread(sent, *holds):
        sent = list(sent)
        got = [sent[0]] + [None] * (chips - 1)
        for step, dist in enumerate(order):
            for at, done in holds:
                if at == step:
                    sent[dist] = after(sent[dist], done())
            got[dist] = lane(sent[dist], dist)
        return got

    def pack(i):
        return pack_momentum(meta, table, momentum6, crossed[i], i, chunk, cap)

    def theta_part(i, part, *done):
        new = step_theta(meta, table, theta4, after(outer, *done), part, i, chunk, cap)
        return new, rep_lane(new)

    def momentum_part(i, own_half, *done):
        block = near[i] if own_half else far[i]
        crossed = swap_core(after(block, *done) if done else block)
        old = made[-1] if made else None
        made.append(step_momentum(meta, held, momentum6, block, crossed, old, i, own_half))
        return made[-1]

    steps = len(order)
    near, far, made, news, got = [], [], [], [], []

    part = spread(pack(0))
    outer, sent = pack_outer(meta, table, after(mine, lane.arrived[-3]), theirs, chips, groups, chunk, cap)

    def first_theta():
        news.append(theta_part(0, part, lane.arrived[-1]))
        return news[0][0]

    got.append(spread(sent[0], (2, first_theta)))

    def joined(i):
        def joining():
            blocks = list(got[i])
            blocks[-1] = after(blocks[-1], lane.arrived[-1])
            near.append(join(blocks))
            far.append(rep_lane(near[i]))
            return near[i]

        return joining

    for i in range(1, count):
        got.append(spread(sent[i], (2, joined(i - 1)), (steps - 1, lambda i=i: momentum_part(i - 1, True))))
    for i in range(1, count):
        holds = [(2, joined(i)), (steps - 2, lambda i=i: momentum_part(i, True))]
        holds.append((steps - 1, lambda i=i: momentum_part(i - 1, False)))
        part = spread(pack(i), *holds)
        news.append(theta_part(i, part))
    if count == 1:
        joined(0)()
        momentum_part(0, True)
    momentum_part(count - 1, False, news[-1][0])
    made = made[-1]

    out = jnp.zeros((mats, groups, half, width), jnp.float32)
    zero = jnp.int32(0)
    for i, (new, other) in enumerate(news):
        out = lax.dynamic_update_slice(out, new[:, None], (zero, rep, jnp.int32(i * chunk), zero))
        out = lax.dynamic_update_slice(out, other[:, None], (zero, 1 - rep, jnp.int32(i * chunk), zero))
    return out.reshape(theta.shape), made.reshape(momentum.shape)


def local(theta, inner, momentum, owner, order):
    owners = lax.axis_size("shard")
    chips = owners // CORES
    mats = theta.shape[0]
    ranks = momentum.shape[0]
    layers, kinds = order.shape
    myself = lax.axis_index("shard")

    ids = jnp.arange(mats, dtype=jnp.int32)
    ident = (kinds * jnp.arange(layers, dtype=jnp.int32)[:, None] + order).reshape(mats)
    owner_at = jnp.sum(jnp.where(ident[:, None] == ids[None, :], owner[None, :], 0), axis=1)
    chip_at = owner_at // CORES
    before = ident[None, :] < ident[:, None]
    same_owner = owner_at[None, :] == owner_at[:, None]
    rank_at = jnp.sum((same_owner & before).astype(jnp.int32), axis=1)
    same_chip = chip_at[None, :] == chip_at[:, None]
    ahead = (owner_at[None, :] < owner_at[:, None]) | (same_owner & before)
    place_at = jnp.sum((same_chip & ahead).astype(jnp.int32), axis=1)
    most = jnp.max(place_at) + 1

    entry = jnp.arange(chips * 4, dtype=jnp.int32)
    hit = entry[:, None] == (chip_at * 4 + place_at)[None, :]
    gather = lambda v: jnp.sum(jnp.where(hit, v[None, :], 0), axis=1)
    table = jnp.stack([gather(ids), gather(rank_at), gather(owner_at % CORES), gather(jnp.ones_like(ids))])

    slot_at = jnp.arange(ranks, dtype=jnp.int32)
    mine = (owner_at[None, :] == myself) & (rank_at[None, :] == slot_at[:, None])
    held = jnp.stack(
        [jnp.sum(jnp.where(mine, place_at[None, :], 0), axis=1), jnp.sum(mine.astype(jnp.int32), axis=1)]
    )
    meta = jnp.stack([myself // CORES, myself % CORES, lax.axis_index("rep")]).astype(jnp.int32)

    caps = list(range(ranks, CORES * ranks + 1))
    branches = [functools.partial(run, cap) for cap in caps]
    which = jnp.clip(most - ranks, 0, len(caps) - 1)
    half = theta.shape[1] // lax.axis_size("rep")
    chunk = half // 2 if half % 16 == 0 else half
    crossed = cross_momentum(momentum, half, chunk)
    return lax.switch(which, branches, theta, inner[0], momentum, crossed, meta, table, held)


def solution(mesh):
    in_specs = (
        P(None, "shard", None),
        P("rep", None, "shard", None),
        P("shard", None, None),
        P(),
        P(),
    )
    out_specs = (P(None, "shard", None), P("shard", None, None))
    return jax.shard_map(local, mesh=mesh, in_specs=in_specs, out_specs=out_specs, check_vma=False)
```

```python
import functools

import jax
import jax.numpy as jnp
from jax import lax
from jax.experimental import pallas as pl
from jax.experimental.pallas import tpu as pltpu
from jax.sharding import PartitionSpec as P

CORES = 2
LANES = 4


def whole(shape):
    return pl.BlockSpec(shape, lambda *_: (0,) * len(shape))


def params(*arrays):
    size = sum(a.size * 4 for a in arrays)
    return pltpu.CompilerParams(vmem_limit_bytes=min(60 << 20, (8 << 20) + 3 * size))


def pack_momentum(meta, table, momentum6, crossed, chunk, rows, cap):
    ranks, chips, _, _, _, width = momentum6.shape

    def kernel(meta_ref, table_ref, own_ref, crossed_ref, *outs):
        chip, core = meta_ref[0], meta_ref[1]
        for slot in range(cap):
            entry = chip * 4 + slot
            rank = table_ref[1, entry]
            mine = table_ref[2, entry] == core
            for dist in range(chips):
                other = chip ^ dist

                @pl.when(mine)
                def _():
                    outs[dist][slot] = own_ref[rank, other, 0, 0]

                @pl.when(jnp.logical_not(mine))
                def _():
                    outs[dist][slot] = crossed_ref[rank, other]

    out = jax.ShapeDtypeStruct((cap, rows, width), jnp.float32)
    own_block = (ranks, chips, 1, 1, rows, width)
    block_at = lambda i, meta_ref, table_ref: (0, 0, meta_ref[1], meta_ref[2], chunk, 0)
    crossed_at = lambda i, meta_ref, table_ref: (0, 0, chunk, 0)
    return pl.pallas_call(
        kernel,
        grid_spec=pltpu.PrefetchScalarGridSpec(
            num_scalar_prefetch=2,
            grid=(1,),
            in_specs=[pl.BlockSpec(own_block, block_at), pl.BlockSpec((ranks, chips, rows, width), crossed_at)],
            out_specs=[whole(out.shape)] * chips,
        ),
        out_shape=[out] * chips,
        compiler_params=params(crossed, crossed, *[out] * chips),
        name="pack_momentum",
    )(meta, table, momentum6, crossed)


def pack_outer(meta, table, mine, theirs, chips, groups, chunk, cap):
    mats, rows, width = mine.shape
    count = rows // chunk

    def kernel(meta_ref, table_ref, mine_ref, theirs_ref, outer_ref, *outs):
        outer_ref[...] = (mine_ref[...] + theirs_ref[...]) / groups
        chip = meta_ref[0]
        for dist in range(chips):
            for slot in range(cap):
                at = table_ref[0, (chip ^ dist) * 4 + slot]
                for i in range(count):
                    outs[i * chips + dist][slot] = outer_ref[at, i * chunk : (i + 1) * chunk]

    out = jax.ShapeDtypeStruct((cap, chunk, width), jnp.float32)
    outer, *sent = pl.pallas_call(
        kernel,
        grid_spec=pltpu.PrefetchScalarGridSpec(
            num_scalar_prefetch=2,
            grid=(1,),
            in_specs=[whole(mine.shape), whole(mine.shape)],
            out_specs=[whole(mine.shape)] + [whole(out.shape)] * (count * chips),
        ),
        out_shape=[jax.ShapeDtypeStruct(mine.shape, jnp.float32)] + [out] * (count * chips),
        compiler_params=params(mine, mine, mine, *[out] * (count * chips)),
        name="pack_outer",
    )(meta, table, mine, theirs)
    return outer, [sent[i * chips : (i + 1) * chips] for i in range(count)]


def join(blocks):
    def kernel(*refs):
        for i in range(len(blocks)):
            refs[-1][i] = refs[i][...]

    block = blocks[0]
    return pl.pallas_call(
        kernel,
        out_shape=jax.ShapeDtypeStruct((len(blocks), *block.shape), jnp.float32),
        in_specs=[pl.BlockSpec(memory_space=pltpu.VMEM)] * len(blocks),
        out_specs=pl.BlockSpec(memory_space=pltpu.VMEM),
        compiler_params=params(*blocks),
        name="join",
    )(*blocks)


def step_theta(meta, table, theta4, outer, blocks, chunk, rows, cap):
    mats, _, _, width = theta4.shape
    chips = len(blocks)

    def kernel(meta_ref, table_ref, theta_ref, outer_ref, *refs):
        out_ref = refs[chips]
        chip = meta_ref[0]
        for dist in range(chips):
            for slot in range(cap):
                entry = (chip ^ dist) * 4 + slot

                @pl.when(table_ref[3, entry] > 0)
                def _():
                    at = table_ref[0, entry]
                    outer_now = outer_ref[at]
                    fresh = 0.5 * refs[dist][slot] + outer_now
                    shifted = theta_ref[at, 0] - 0.7 * (outer_now + 0.5 * fresh)
                    mean = jnp.mean(shifted * shifted, axis=-1, keepdims=True)
                    out_ref[at] = shifted / jnp.sqrt(mean + 1e-06)

    out = jax.ShapeDtypeStruct((mats, rows, width), jnp.float32)
    return pl.pallas_call(
        kernel,
        grid_spec=pltpu.PrefetchScalarGridSpec(
            num_scalar_prefetch=2,
            grid=(1,),
            in_specs=[
                pl.BlockSpec((mats, 1, rows, width), lambda i, meta_ref, table_ref: (0, meta_ref[2], chunk, 0)),
                pl.BlockSpec((mats, rows, width), lambda i, meta_ref, table_ref: (0, chunk, 0)),
            ]
            + [whole((cap, rows, width))] * chips,
            out_specs=whole(out.shape),
        ),
        out_shape=out,
        compiler_params=params(out, out, out, *blocks),
        name="step_theta",
    )(meta, table, theta4, outer, *blocks)


def step_momentum(meta, held, momentum6, near, far, old, chunk, own_half):
    ranks, chips, _, _, _, width = momentum6.shape
    rows = near.shape[2]

    def kernel(meta_ref, held_ref, momentum_ref, near_ref, far_ref, *refs):
        out_ref = refs[-1]
        chip, core = meta_ref[0], meta_ref[1]
        used = held_ref[1, pl.program_id(0)] > 0

        @pl.when(used)
        def _():
            for at in range(chips):
                for place, ref in ((core, near_ref), (1 - core, far_ref)):
                    out_ref[0, at, place, 0] = 0.5 * momentum_ref[0, at, place, 0] + ref[at ^ chip, 0]

        @pl.when(jnp.logical_not(used))
        def _():
            out_ref[...] = momentum_ref[...]

    def big_at(k, meta_ref, held_ref):
        return k, 0, 0, meta_ref[2] if own_half else 1 - meta_ref[2], chunk, 0

    big = pl.BlockSpec((1, chips, CORES, 1, rows, width), big_at)
    small = pl.BlockSpec((chips, 1, rows, width), lambda k, meta_ref, held_ref: (0, held_ref[0, k], 0, 0))
    extra = [] if old is None else [old]
    size = chips * CORES * rows * width * 4
    return pl.pallas_call(
        kernel,
        grid_spec=pltpu.PrefetchScalarGridSpec(
            num_scalar_prefetch=2,
            grid=(ranks,),
            in_specs=[big, small, small] + [pl.BlockSpec(memory_space=pl.ANY)] * len(extra),
            out_specs=big,
        ),
        out_shape=pltpu.HBM(momentum6.shape, jnp.float32),
        input_output_aliases={5: 0} if extra else {},
        compiler_params=pltpu.CompilerParams(vmem_limit_bytes=(8 << 20) + 6 * size),
        cost_estimate=pl.CostEstimate(flops=ranks * size, bytes_accessed=3 * ranks * size, transcendentals=0),
        name="step_momentum",
    )(meta, held, momentum6, near, far, *extra)


def swap_core(x):
    owners = lax.axis_size("shard")
    with jax.named_scope("swap_core"):
        return lax.ppermute(x, "shard", [(s, s ^ 1) for s in range(owners)])


def cross_momentum(momentum6):
    ranks, chips, _, _, rows, width = momentum6.shape
    other = 1 - lax.axis_index("shard") % CORES
    start = (0, 0, other, lax.axis_index("rep"), 0, 0)
    part = lax.dynamic_slice(momentum6, start, (ranks, chips, 1, 1, rows, width))
    return swap_core(part.reshape(ranks, chips, rows, width))


def after(x, *done):
    return lax.optimization_barrier((x, *done))[0]


class Lane:
    def __init__(self, window, send):
        self.window, self.send, self.arrived = window, send, []

    def __call__(self, x, *args):
        if len(self.arrived) >= self.window:
            x = after(x, self.arrived[-self.window])
        self.arrived.append(self.send(x, *args))
        return self.arrived[-1]


def lane_order(chips):
    long, short = list(range(chips // 2, chips)), list(range(1, chips // 2))
    order = []
    while long:
        a, b, c, d = long[:LANES]
        x, y, z = short[: LANES - 1]
        order += [(0, a), (1, y), (2, c), (3, d), (0, x), (1, b), (2, z)]
        long, short = long[LANES:], short[LANES - 1 :]
    return order + [(i % LANES, dist) for i, dist in enumerate(short)]


def run(cap, theta, inner, momentum6, crossed, meta, table, held):
    groups = lax.axis_size("rep")
    owners = lax.axis_size("shard")
    chips = owners // CORES
    mats, rows, width = theta.shape
    half = rows // groups
    rep = lax.axis_index("rep")

    def swap_rep(x):
        with jax.named_scope("swap_rep"):
            return lax.ppermute(x, "rep", [(g, g ^ 1) for g in range(groups)])

    def swap_chip(x, dist):
        with jax.named_scope(f"swap_chip_{dist}"):
            return lax.ppermute(x, "shard", [(s, s ^ (CORES * dist)) for s in range(owners)])

    lanes = [Lane(1, swap_chip) for _ in range(LANES)]
    rep_lane = Lane(1, swap_rep)
    order = lane_order(chips)

    theta4 = theta.reshape(mats, groups, half, width)
    inner4 = inner.reshape(mats, groups, half, width)
    chunk = half // 2 if half % 16 == 0 else half
    count = half // chunk

    def diff(at):
        pick = lambda a: lax.dynamic_index_in_dim(a, at, 1, keepdims=False)
        return pick(theta4) - pick(inner4).astype(jnp.float32)

    theirs = rep_lane(diff(1 - rep))
    mine = diff(rep)

    def spread(sent, *holds):
        sent = list(sent)
        got = [sent[0]] + [None] * (chips - 1)
        for at, (lane, dist) in enumerate(order):
            for place, done in holds:
                if place == at:
                    sent[dist] = after(sent[dist], done())
            got[dist] = lanes[lane](sent[dist], dist)
        return got

    def pack(i):
        return pack_momentum(meta, table, momentum6, crossed, i, chunk, cap)

    def theta_part(i, part, send):
        new = step_theta(meta, table, theta4, outer, part, i, chunk, cap)
        return new, send(new)

    def momentum_part(i, own_half, *done):
        block = near[i] if own_half else far[i]
        crossed = swap_core(after(block, *done) if done else block)
        old = made[-1] if made else None
        made.append(step_momentum(meta, held, momentum6, block, crossed, old, i, own_half))
        return made[-1]

    near, far, made, news, got = [], [], [], [], []

    packed = []

    def packing(i):
        def pack_now():
            packed.append(pack(i))
            return packed[-1][0]

        return pack_now

    part = spread(pack(0))
    outer, sent = pack_outer(meta, table, after(mine, lanes[1].arrived[0]), theirs, chips, groups, chunk, cap)

    def first_theta():
        news.append(theta_part(0, part, rep_lane))
        return news[0][0]

    def joined(i):
        def joining():
            near.append(join(got[i]))
            far.append(rep_lane(near[i]))
            return near[i]

        return joining

    got.append(spread(sent[0], (4, first_theta), (6, lambda: news[0][1]), *((6, packing(i)) for i in range(1, count))))
    for i in range(1, count):
        got.append(spread(sent[i], (5, joined(i - 1))))
    for i in range(1, count):
        part = spread(packed[i - 1], (5, joined(i)))
        news.append(theta_part(i, part, rep_lane))
    if count == 1:
        joined(0)()
    for own_half in (True, False):
        for i in range(count):
            momentum_part(i, own_half, news[-1][0])
    made = made[-1]

    out = jnp.zeros((mats, groups, half, width), jnp.float32)
    zero = jnp.int32(0)
    news[-1] = news[-1][0], after(news[-1][1], made)
    for i, (new, other) in enumerate(news):
        out = lax.dynamic_update_slice(out, new[:, None], (zero, rep, jnp.int32(i * chunk), zero))
        out = lax.dynamic_update_slice(out, other[:, None], (zero, 1 - rep, jnp.int32(i * chunk), zero))
    return out.reshape(theta.shape), made


def local(theta, inner, momentum, owner, order):
    owners = lax.axis_size("shard")
    chips = owners // CORES
    mats = theta.shape[0]
    ranks = momentum.shape[0]
    layers, kinds = order.shape
    myself = lax.axis_index("shard")

    ids = jnp.arange(mats, dtype=jnp.int32)
    ident = (kinds * jnp.arange(layers, dtype=jnp.int32)[:, None] + order).reshape(mats)
    owner_at = jnp.sum(jnp.where(ident[:, None] == ids[None, :], owner[None, :], 0), axis=1)
    chip_at = owner_at // CORES
    before = ident[None, :] < ident[:, None]
    same_owner = owner_at[None, :] == owner_at[:, None]
    rank_at = jnp.sum((same_owner & before).astype(jnp.int32), axis=1)
    same_chip = chip_at[None, :] == chip_at[:, None]
    ahead = (owner_at[None, :] < owner_at[:, None]) | (same_owner & before)
    place_at = jnp.sum((same_chip & ahead).astype(jnp.int32), axis=1)
    most = jnp.max(place_at) + 1

    entry = jnp.arange(chips * 4, dtype=jnp.int32)
    hit = entry[:, None] == (chip_at * 4 + place_at)[None, :]
    gather = lambda v: jnp.sum(jnp.where(hit, v[None, :], 0), axis=1)
    table = jnp.stack([gather(ids), gather(rank_at), gather(owner_at % CORES), gather(jnp.ones_like(ids))])

    slot_at = jnp.arange(ranks, dtype=jnp.int32)
    mine = (owner_at[None, :] == myself) & (rank_at[None, :] == slot_at[:, None])
    held = jnp.stack(
        [jnp.sum(jnp.where(mine, place_at[None, :], 0), axis=1), jnp.sum(mine.astype(jnp.int32), axis=1)]
    )
    meta = jnp.stack([myself // CORES, myself % CORES, lax.axis_index("rep")]).astype(jnp.int32)

    caps = list(range(ranks, CORES * ranks + 1))
    branches = [functools.partial(run, cap) for cap in caps]
    which = jnp.clip(most - ranks, 0, len(caps) - 1)
    half = theta.shape[1] // lax.axis_size("rep")
    momentum6 = momentum.reshape(ranks, chips, CORES, lax.axis_size("rep"), half, momentum.shape[2])
    crossed = cross_momentum(momentum6)
    theta, momentum = lax.switch(which, branches, theta, inner[0], momentum6, crossed, meta, table, held)
    return theta, momentum.reshape(ranks, *momentum.shape[-1:] * 2)


def solution(mesh):
    in_specs = (
        P(None, "shard", None),
        P("rep", None, "shard", None),
        P("shard", None, None),
        P(),
        P(),
    )
    out_specs = (P(None, "shard", None), P("shard", None, None))
    return jax.shard_map(local, mesh=mesh, in_specs=in_specs, out_specs=out_specs, check_vma=False)
```

```python
import functools

import jax
import jax.numpy as jnp
from jax import lax
from jax.experimental import pallas as pl
from jax.experimental.pallas import tpu as pltpu
from jax.sharding import PartitionSpec as P

CORES = 2
LANES = 4


def whole(shape):
    return pl.BlockSpec(shape, lambda *_: (0,) * len(shape))


def params(*arrays):
    size = sum(a.size * 4 for a in arrays)
    return pltpu.CompilerParams(vmem_limit_bytes=min(60 << 20, (8 << 20) + 3 * size))


def pack_momentum(meta, table, momentum6, crossed, chunk, rows, cap):
    ranks, chips, _, _, _, width = momentum6.shape

    def kernel(meta_ref, table_ref, own_ref, crossed_ref, *outs):
        chip, core = meta_ref[0], meta_ref[1]
        for slot in range(cap):
            entry = chip * 4 + slot
            rank = table_ref[1, entry]
            mine = table_ref[2, entry] == core
            for dist in range(chips):
                other = chip ^ dist

                @pl.when(mine)
                def _():
                    outs[dist][slot] = own_ref[rank, other, 0, 0]

                @pl.when(jnp.logical_not(mine))
                def _():
                    outs[dist][slot] = crossed_ref[rank, other]

    out = jax.ShapeDtypeStruct((cap, rows, width), jnp.float32)
    own_block = (ranks, chips, 1, 1, rows, width)
    block_at = lambda i, meta_ref, table_ref: (0, 0, meta_ref[1], meta_ref[2], chunk, 0)
    crossed_at = lambda i, meta_ref, table_ref: (0, 0, chunk, 0)
    return pl.pallas_call(
        kernel,
        grid_spec=pltpu.PrefetchScalarGridSpec(
            num_scalar_prefetch=2,
            grid=(1,),
            in_specs=[pl.BlockSpec(own_block, block_at), pl.BlockSpec((ranks, chips, rows, width), crossed_at)],
            out_specs=[whole(out.shape)] * chips,
        ),
        out_shape=[out] * chips,
        compiler_params=params(crossed, crossed, *[out] * chips),
        name="pack_momentum",
    )(meta, table, momentum6, crossed)


def pack_outer(meta, table, mine, theirs, chips, groups, chunk, cap):
    mats, rows, width = mine.shape
    count = rows // chunk

    def kernel(meta_ref, table_ref, mine_ref, theirs_ref, outer_ref, *outs):
        outer_ref[...] = (mine_ref[...] + theirs_ref[...]) / groups
        chip = meta_ref[0]
        for dist in range(chips):
            for slot in range(cap):
                at = table_ref[0, (chip ^ dist) * 4 + slot]
                for i in range(count):
                    outs[i * chips + dist][slot] = outer_ref[at, i * chunk : (i + 1) * chunk]

    out = jax.ShapeDtypeStruct((cap, chunk, width), jnp.float32)
    outer, *sent = pl.pallas_call(
        kernel,
        grid_spec=pltpu.PrefetchScalarGridSpec(
            num_scalar_prefetch=2,
            grid=(1,),
            in_specs=[whole(mine.shape), whole(mine.shape)],
            out_specs=[whole(mine.shape)] + [whole(out.shape)] * (count * chips),
        ),
        out_shape=[jax.ShapeDtypeStruct(mine.shape, jnp.float32)] + [out] * (count * chips),
        compiler_params=params(mine, mine, mine, *[out] * (count * chips)),
        name="pack_outer",
    )(meta, table, mine, theirs)
    return outer, [sent[i * chips : (i + 1) * chips] for i in range(count)]


def join(blocks):
    def kernel(*refs):
        for i in range(len(blocks)):
            refs[-1][i] = refs[i][...]

    block = blocks[0]
    return pl.pallas_call(
        kernel,
        out_shape=jax.ShapeDtypeStruct((len(blocks), *block.shape), jnp.float32),
        in_specs=[pl.BlockSpec(memory_space=pltpu.VMEM)] * len(blocks),
        out_specs=pl.BlockSpec(memory_space=pltpu.VMEM),
        compiler_params=params(*blocks),
        name="join",
    )(*blocks)


def step_theta(meta, table, theta4, outer, blocks, chunk, rows, cap):
    mats, _, _, width = theta4.shape
    chips = len(blocks)

    def kernel(meta_ref, table_ref, theta_ref, outer_ref, *refs):
        out_ref = refs[chips]
        chip = meta_ref[0]
        for dist in range(chips):
            for slot in range(cap):
                entry = (chip ^ dist) * 4 + slot

                @pl.when(table_ref[3, entry] > 0)
                def _():
                    at = table_ref[0, entry]
                    outer_now = outer_ref[at]
                    fresh = 0.5 * refs[dist][slot] + outer_now
                    shifted = theta_ref[at, 0] - 0.7 * (outer_now + 0.5 * fresh)
                    mean = jnp.mean(shifted * shifted, axis=-1, keepdims=True)
                    out_ref[at] = shifted / jnp.sqrt(mean + 1e-06)

    out = jax.ShapeDtypeStruct((mats, rows, width), jnp.float32)
    return pl.pallas_call(
        kernel,
        grid_spec=pltpu.PrefetchScalarGridSpec(
            num_scalar_prefetch=2,
            grid=(1,),
            in_specs=[
                pl.BlockSpec((mats, 1, rows, width), lambda i, meta_ref, table_ref: (0, meta_ref[2], chunk, 0)),
                pl.BlockSpec((mats, rows, width), lambda i, meta_ref, table_ref: (0, chunk, 0)),
            ]
            + [whole((cap, rows, width))] * chips,
            out_specs=whole(out.shape),
        ),
        out_shape=out,
        compiler_params=params(out, out, out, *blocks),
        name="step_theta",
    )(meta, table, theta4, outer, *blocks)


def step_momentum(meta, held, momentum6, blocks, old, chunk):
    ranks, chips, _, groups, _, width = momentum6.shape
    rows = blocks[0].shape[2]

    def kernel(meta_ref, held_ref, momentum_ref, *refs):
        out_ref = refs[-1]
        chip, core, rep = meta_ref[0], meta_ref[1], meta_ref[2]
        used = held_ref[1, pl.program_id(0)] > 0

        @pl.when(used)
        def _():
            for i in range(len(blocks)):
                place, half = (1 - core if i % 2 else core), (1 - rep if i // 2 else rep)
                for at in range(chips):
                    out_ref[0, at, place, half] = 0.5 * momentum_ref[0, at, place, half] + refs[i][at ^ chip, 0]

        @pl.when(jnp.logical_not(used))
        def _():
            out_ref[...] = momentum_ref[...]

    big = pl.BlockSpec(
        (1, chips, CORES, groups, rows, width), lambda k, meta_ref, held_ref: (k, 0, 0, 0, chunk, 0)
    )
    small = pl.BlockSpec((chips, 1, rows, width), lambda k, meta_ref, held_ref: (0, held_ref[0, k], 0, 0))
    extra = [] if old is None else [old]
    size = chips * CORES * groups * rows * width * 4
    return pl.pallas_call(
        kernel,
        grid_spec=pltpu.PrefetchScalarGridSpec(
            num_scalar_prefetch=2,
            grid=(ranks,),
            in_specs=[big] + [small] * len(blocks) + [pl.BlockSpec(memory_space=pl.ANY)] * len(extra),
            out_specs=big,
        ),
        out_shape=pltpu.HBM(momentum6.shape, jnp.float32),
        input_output_aliases={3 + len(blocks): 0} if extra else {},
        compiler_params=pltpu.CompilerParams(vmem_limit_bytes=(8 << 20) + 6 * size),
        cost_estimate=pl.CostEstimate(flops=ranks * size, bytes_accessed=3 * ranks * size, transcendentals=0),
        name="step_momentum",
    )(meta, held, momentum6, *blocks, *extra)


def swap_core(x):
    owners = lax.axis_size("shard")
    with jax.named_scope("swap_core"):
        return lax.ppermute(x, "shard", [(s, s ^ 1) for s in range(owners)])


def cross_momentum(momentum6):
    ranks, chips, _, _, rows, width = momentum6.shape
    other = 1 - lax.axis_index("shard") % CORES
    start = (0, 0, other, lax.axis_index("rep"), 0, 0)
    part = lax.dynamic_slice(momentum6, start, (ranks, chips, 1, 1, rows, width))
    return swap_core(part.reshape(ranks, chips, rows, width))


def after(x, *done):
    return lax.optimization_barrier((x, *done))[0]


class Lane:
    def __init__(self, window, send):
        self.window, self.send, self.arrived = window, send, []

    def __call__(self, x, *args):
        if len(self.arrived) >= self.window:
            x = after(x, self.arrived[-self.window])
        self.arrived.append(self.send(x, *args))
        return self.arrived[-1]


def lane_order(chips):
    long, short = list(range(chips // 2, chips)), list(range(1, chips // 2))
    order = []
    while long:
        a, b, c, d = long[:LANES]
        x, y, z = short[: LANES - 1]
        order += [(0, a), (1, y), (2, c), (3, d), (0, x), (1, b), (2, z)]
        long, short = long[LANES:], short[LANES - 1 :]
    return order + [(i % LANES, dist) for i, dist in enumerate(short)]


def run(cap, theta, inner, momentum6, crossed, meta, table, held):
    groups = lax.axis_size("rep")
    owners = lax.axis_size("shard")
    chips = owners // CORES
    mats, rows, width = theta.shape
    half = rows // groups
    rep = lax.axis_index("rep")

    def swap_rep(x):
        with jax.named_scope("swap_rep"):
            return lax.ppermute(x, "rep", [(g, g ^ 1) for g in range(groups)])

    def swap_chip(x, dist):
        with jax.named_scope(f"swap_chip_{dist}"):
            return lax.ppermute(x, "shard", [(s, s ^ (CORES * dist)) for s in range(owners)])

    lanes = [Lane(1, swap_chip) for _ in range(LANES)]
    rep_lane = Lane(1, swap_rep)
    order = lane_order(chips)

    theta4 = theta.reshape(mats, groups, half, width)
    inner4 = inner.reshape(mats, groups, half, width)
    chunk = half // 2 if half % 16 == 0 else half
    count = half // chunk

    def diff(at):
        pick = lambda a: lax.dynamic_index_in_dim(a, at, 1, keepdims=False)
        return pick(theta4) - pick(inner4).astype(jnp.float32)

    theirs = rep_lane(diff(1 - rep))
    mine = diff(rep)

    def spread(sent, *holds):
        sent = list(sent)
        got = [sent[0]] + [None] * (chips - 1)
        for at, (lane, dist) in enumerate(order):
            for place, done in holds:
                if place == at:
                    sent[dist] = after(sent[dist], done())
            got[dist] = lanes[lane](sent[dist], dist)
        return got

    def pack(i):
        return pack_momentum(meta, table, momentum6, crossed, i, chunk, cap)

    def theta_part(i, part, send):
        new = step_theta(meta, table, theta4, outer, part, i, chunk, cap)
        return new, send(new)

    def momentum_part(i, *done):
        blocks = [near[i], swap_core(after(near[i], *done)), far[i], swap_core(after(far[i], *done))]
        made.append(step_momentum(meta, held, momentum6, blocks, made[-1] if made else None, i))

    near, far, made, news, got = [], [], [], [], []

    packed = []

    def packing(i):
        def pack_now():
            packed.append(pack(i))
            return packed[-1][0]

        return pack_now

    part = spread(pack(0))
    outer, sent = pack_outer(meta, table, after(mine, lanes[1].arrived[0]), theirs, chips, groups, chunk, cap)

    def first_theta():
        news.append(theta_part(0, part, rep_lane))
        return news[0][0]

    def joined(i):
        def joining():
            near.append(join(got[i]))
            far.append(rep_lane(near[i]))
            return near[i]

        return joining

    got.append(spread(sent[0], (4, first_theta), (6, lambda: news[0][1]), *((6, packing(i)) for i in range(1, count))))
    for i in range(1, count):
        got.append(spread(sent[i], (5, joined(i - 1))))
    for i in range(1, count):
        part = spread(packed[i - 1], (5, joined(i)))
        news.append(theta_part(i, part, rep_lane))
    if count == 1:
        joined(0)()
    for i in range(count):
        momentum_part(i, news[-1][0])
    made = made[-1]

    out = jnp.zeros((mats, groups, half, width), jnp.float32)
    zero = jnp.int32(0)
    news[-1] = news[-1][0], after(news[-1][1], made)
    for i, (new, other) in enumerate(news):
        out = lax.dynamic_update_slice(out, new[:, None], (zero, rep, jnp.int32(i * chunk), zero))
        out = lax.dynamic_update_slice(out, other[:, None], (zero, 1 - rep, jnp.int32(i * chunk), zero))
    return out.reshape(theta.shape), made


def local(theta, inner, momentum, owner, order):
    owners = lax.axis_size("shard")
    chips = owners // CORES
    mats = theta.shape[0]
    ranks = momentum.shape[0]
    layers, kinds = order.shape
    myself = lax.axis_index("shard")

    ids = jnp.arange(mats, dtype=jnp.int32)
    ident = (kinds * jnp.arange(layers, dtype=jnp.int32)[:, None] + order).reshape(mats)
    owner_at = jnp.sum(jnp.where(ident[:, None] == ids[None, :], owner[None, :], 0), axis=1)
    chip_at = owner_at // CORES
    before = ident[None, :] < ident[:, None]
    same_owner = owner_at[None, :] == owner_at[:, None]
    rank_at = jnp.sum((same_owner & before).astype(jnp.int32), axis=1)
    same_chip = chip_at[None, :] == chip_at[:, None]
    ahead = (owner_at[None, :] < owner_at[:, None]) | (same_owner & before)
    place_at = jnp.sum((same_chip & ahead).astype(jnp.int32), axis=1)
    most = jnp.max(place_at) + 1

    entry = jnp.arange(chips * 4, dtype=jnp.int32)
    hit = entry[:, None] == (chip_at * 4 + place_at)[None, :]
    gather = lambda v: jnp.sum(jnp.where(hit, v[None, :], 0), axis=1)
    table = jnp.stack([gather(ids), gather(rank_at), gather(owner_at % CORES), gather(jnp.ones_like(ids))])

    slot_at = jnp.arange(ranks, dtype=jnp.int32)
    mine = (owner_at[None, :] == myself) & (rank_at[None, :] == slot_at[:, None])
    held = jnp.stack(
        [jnp.sum(jnp.where(mine, place_at[None, :], 0), axis=1), jnp.sum(mine.astype(jnp.int32), axis=1)]
    )
    meta = jnp.stack([myself // CORES, myself % CORES, lax.axis_index("rep")]).astype(jnp.int32)

    caps = list(range(ranks, CORES * ranks + 1))
    branches = [functools.partial(run, cap) for cap in caps]
    which = jnp.clip(most - ranks, 0, len(caps) - 1)
    half = theta.shape[1] // lax.axis_size("rep")
    momentum6 = momentum.reshape(ranks, chips, CORES, lax.axis_size("rep"), half, momentum.shape[2])
    crossed = cross_momentum(momentum6)
    theta, momentum = lax.switch(which, branches, theta, inner[0], momentum6, crossed, meta, table, held)
    return theta, momentum.reshape(ranks, *momentum.shape[-1:] * 2)


def solution(mesh):
    in_specs = (
        P(None, "shard", None),
        P("rep", None, "shard", None),
        P("shard", None, None),
        P(),
        P(),
    )
    out_specs = (P(None, "shard", None), P("shard", None, None))
    return jax.shard_map(local, mesh=mesh, in_specs=in_specs, out_specs=out_specs, check_vma=False)
```
